256 devices in a mesh: row: 32 (over z_lo, y, x), col: 8 (over z_hi, core).
Axes of the slice: x: 4, y: 4, z: 8 (z_hi: 4, z_lo: 2; z = z_hi * 2 + z_lo), core: 2. Of those that a mesh axis runs over, the one named last changes fastest.
Arguments:
- counts: int32 [32, 8], P('row', 'col'), may hold values from 16 to 159
- inputs: bfloat16 [32, 8, 512, 2048], P('row', 'col'), may hold values from -6 to 6
- cotangent: bfloat16 [32, 8, 512, 1024], P('row', 'col'), may hold values from -0.625 to 0.625
- delta_two: bfloat16 [32, 8, 1024, 2048], P('row', 'col'), may hold values from -6 to 6
- moment_one: float32 [8, 2048, 1024], P('col', 'row'), may hold values from -3 to 3
- moment_two: float32 [32, 1024, 2048], P('row', None, 'col'), may hold values from -3 to 3
Outputs:
- step_one: float32 [8, 2048, 1024], P('col', 'row')
- moment_one_new: float32 [8, 2048, 1024], P('col', 'row')
- step_two: float32 [32, 1024, 2048], P('row', None, 'col')
- moment_two_new: float32 [32, 1024, 2048], P('row', None, 'col')
The draws below stay inside these ranges and needn't reach their ends.
All inputs are finite; a program needn't handle non-finite values.
Results may differ from the reference program's by a relative error of at most 0.0003.
Values sent between devices are 32-bit elements; how exact they have to be, the bound alone decides.
No kernel may reach another device: no remote copies, remote signals or barrier semaphores. Data moves between devices by JAX's collectives and lax.ppermute only.
A program may use at most 128 MiB of HBM per device.

```python
import jax
import jax.numpy as jnp
from jax import lax

D = 2048
H = 1024
TOK_DEV = 512
PATH_ROWS = 32
PATH_COLS = 8
N_ROW = 32
N_COL = 8


def draw_counts(key, part):
    key = jax.random.fold_in(key, 11)
    row_at = lax.broadcasted_iota(jnp.int32, (PATH_ROWS, PATH_COLS), 0)
    col_at = lax.broadcasted_iota(jnp.int32, (PATH_ROWS, PATH_COLS), 1)
    base = (16 + 32 * row_at // (PATH_ROWS - 1)) * (16 + 32 * col_at // (PATH_COLS - 1)) // 16
    return base + jax.random.randint(key, (PATH_ROWS, PATH_COLS), 0, 16, jnp.int32)


def raised(drawn, own_key, source, target, parts, factor):
    def block_of(dim):
        return (jnp.arange(drawn.shape[dim]) // (drawn.shape[dim] // parts)).reshape((-1,) + (1,) * (drawn.ndim - 1 - dim))

    one_side = jax.random.permutation(own_key, parts)[block_of(target)]
    far = (block_of(target) + parts // 2) % parts
    return jnp.where((block_of(source) == one_side) | (block_of(source) == far), factor * drawn, drawn)


def steps_of(stream_key, dims, cuts, smallest, top_value):
    def one(axis_at, blocks):
        draws = jax.random.uniform(jax.random.fold_in(jax.random.fold_in(stream_key, 6), axis_at), (blocks,), jnp.float32, smallest / len(cuts), top_value / len(cuts))
        return jnp.repeat(jnp.exp(draws), dims[axis_at] // blocks).reshape((-1,) + (1,) * (len(dims) - axis_at - 1))

    factor_of = one(*cuts[0])
    for cut in cuts[1:]:
        factor_of = factor_of * one(*cut)
    return factor_of


def bell_draw(key, dims, spread, reach, pieces=(), kind=jnp.bfloat16):
    level = steps_of(key, dims, pieces, -0.22, 0.18) if pieces else 1.0
    result = jax.random.normal(key, dims, jnp.float32) * spread * level
    return jnp.minimum(jnp.maximum(result, -reach), reach).astype(kind)


def bell_draw_with(key, extent, spread, reach, pieces, heavy, kind=jnp.bfloat16):
    drawn = spread * jax.random.normal(key, extent, jnp.float32)
    if pieces:
        drawn = drawn * steps_of(key, extent, pieces, -0.22, 0.18)
    return jnp.clip(raised(drawn, jax.random.fold_in(key, 3), *heavy), -reach, reach).astype(kind)


def setup_inputs(seed: int = 0) -> dict:
    arg_keys = jax.random.split(jax.random.key(seed), 7)
    return {
        "counts": draw_counts(jax.random.fold_in(arg_keys[6], 71), 0),
        "inputs": bell_draw_with(arg_keys[1], (PATH_ROWS, PATH_COLS, TOK_DEV, D), 1.0, 6.0, ((0, 32), (1, 8)), (0, 3, 32, 2.75)),
        "cotangent": bell_draw(arg_keys[2], (PATH_ROWS, PATH_COLS, TOK_DEV, H), (TOK_DEV ** -0.5), 0.625, ((0, 32), (1, 8))),
        "delta_two": bell_draw_with(arg_keys[3], (PATH_ROWS, PATH_COLS, H, D), 1.0, 6.0, ((0, 32), (1, 8)), (1, 3, 8, 2.0)),
        "moment_one": bell_draw(arg_keys[4], (PATH_COLS, D, H), 0.2, 3.0, ((0, 8), (1, 32)), jnp.float32),
        "moment_two": bell_draw(arg_keys[5], (PATH_ROWS, H, D), 0.2, 3.0, ((0, 32), (2, 8)), jnp.float32),
    }


def reference(counts, inputs, cotangent, delta_two, moment_one, moment_two):
    weight = counts.astype(jnp.float32)

    def column(col_at):
        def add_term(total, row_at):
            grad = lax.dot_general(inputs[row_at, col_at], cotangent[row_at, col_at], (((0,), (0,)), ((), ())), preferred_element_type=jnp.float32)
            return total + weight[row_at, col_at] * grad, None
        start = jnp.zeros((D, H), jnp.float32)
        total, unused = lax.scan(add_term, start, jnp.arange(N_ROW, dtype=jnp.int32))
        return total

    sum_one = lax.map(column, jnp.arange(N_COL, dtype=jnp.int32))

    def row_sum(row_at):
        def add_term(total, col_at):
            return total + weight[row_at, col_at] * delta_two[row_at, col_at].astype(jnp.float32), None
        start = jnp.zeros((H, D), jnp.float32)
        total, unused = lax.scan(add_term, start, jnp.arange(N_COL, dtype=jnp.int32))
        return total

    sum_two = lax.map(row_sum, jnp.arange(N_ROW, dtype=jnp.int32))
    total_one = jnp.sum(weight, axis=0)
    total_two = jnp.sum(weight, axis=1)
    mean_one = sum_one / total_one[:, None, None]
    mean_two = sum_two / total_two[:, None, None]
    moment_one_new = 0.9 * moment_one + mean_one
    step_one = 0.7 * (mean_one + 0.9 * moment_one_new)
    moment_two_new = 0.9 * moment_two + mean_two
    step_two = 0.7 * (mean_two + 0.9 * moment_two_new)
    return (step_one, moment_one_new, step_two, moment_two_new)
```

```python
import jax
import jax.numpy as jnp
from jax import lax
from jax.experimental import pallas as pl
from jax.experimental.pallas import tpu as pltpu
from jax.sharding import Mesh, PartitionSpec as P

AXES = ("zlo", "y", "x", "zhi", "core")
SIZES = (2, 4, 4, 4, 2)
F32 = jnp.float32
EXTRA = 8


def permutation(shift):
    pairs = []
    for at in range(256):
        left, place = at, {}
        for name, size in zip(AXES[::-1], SIZES[::-1]):
            left, place[name] = divmod(left, size)
        step = shift(place["core"])
        to = 0
        for name, size in zip(AXES, SIZES):
            to = to * size + (place[name] + step.get(name, 0)) % size
        pairs.append((at, to))
    return pairs


def send(value, shift):
    return lax.ppermute(value, AXES, permutation(shift))


def forward(name):
    return lambda core: {name: 1 if core == 0 else -1}


def backward(name):
    return lambda core: {name: -1 if core == 0 else 1}


def along(name, step):
    return lambda core: {name: step}


def call(body, name, shapes, at, counts, *arrays, after=(), scratch=(), hbm=()):
    n, held = len(arrays) + len(hbm), len(after)

    def kernel(at_ref, counts_ref, *refs):
        body(at_ref, counts_ref[0, 0].astype(F32), *refs[:n], *refs[n + held :])

    smem, vmem, hbm_, anywhere = (pl.BlockSpec(memory_space=s) for s in (pltpu.SMEM, pltpu.VMEM, pltpu.HBM, pl.ANY))
    out = pl.pallas_call(
        kernel,
        in_specs=[smem, smem] + [vmem] * len(arrays) + [hbm_] * len(hbm) + [anywhere] * held,
        out_specs=[vmem] * len(shapes),
        out_shape=[jax.ShapeDtypeStruct(s, F32) for s in shapes],
        scratch_shapes=scratch,
        compiler_params=pltpu.CompilerParams(vmem_limit_bytes=24 << 20),
        cost_estimate=pl.CostEstimate(flops=0, bytes_accessed=3 << 20, transcendentals=0),
        name=name,
    )(at, counts, *arrays, *hbm, *after)
    return out[0] if len(shapes) == 1 else out


def sign_of(at):
    return 1 - 2 * at[1]


def place(at, kind, axis):
    here = at[axis]
    return {"A": here + 2, "B": here + 4 - sign_of(at), "C": here + 4 + sign_of(at), "O": here}[kind] & 3


def column(at, kind, mine):
    core, sign = at[1], sign_of(at)
    if not mine:
        core, sign = 1 - core, -sign
    step, of = {"A": (2, 1 - core), "B": (sign, core), "C": (sign, 1 - core), "O": (0, core)}[kind]
    block = ((at[0] + 4 + step) & 3) * 2 + of
    return pl.ds(pl.multiple_of(block * 256, 256), 256)


ROWS = 1024 + EXTRA


def first_pair_kernel(at, weight, delta, out, blocks, sems):
    copies = [
        pltpu.make_async_copy(delta.at[:, column(at, kind, False)], blocks.at[i], sems.at[i])
        for i, kind in enumerate("AB")
    ]
    for copy in copies:
        copy.start()
    for i, copy in enumerate(copies):
        base = i * ROWS
        out[base + 1024 : base + ROWS, :] = jnp.full((EXTRA, 256), weight, F32)
        copy.wait()
        out[base : base + 1024, :] = weight * blocks[i].astype(F32)


def pair_kernel(at, weight, delta, out):
    for i, kind in enumerate("CO"):
        base = i * ROWS
        out[base : base + 1024, :] = weight * delta[:, column(at, kind, False)].astype(F32)
        out[base + 1024 : base + ROWS, :] = jnp.full((EXTRA, 256), weight, F32)


def add_block(out, to, at, weight, delta, kind, pair, base, got=None, got_base=0):
    total = weight * delta[:, column(at, kind, True)].astype(F32) + pair[base : base + 1024, :]
    weights = weight + pair[base + 1024 : base + ROWS, :]
    if got is not None:
        total += got[got_base : got_base + 1024, :]
        weights += got[got_base + 1024 : got_base + ROWS, :]
    out[to : to + 1024, :] = total
    out[to + 1024 : to + ROWS, :] = weights


def z_first_kernel(at, weight, delta, pair, out):
    add_block(out, 0, at, weight, delta, "A", pair, 0)
    add_block(out, ROWS, at, weight, delta, "B", pair, ROWS)


def z_last_kernel(at, weight, delta, pair, got, last, own):
    add_block(last, 0, at, weight, delta, "C", pair, 0, got, 0)
    add_block(own, 0, at, weight, delta, "O", pair, ROWS, got, ROWS)


def finish_two_kernel(at, weight, part, last, moment, step_out, moment_out):
    total = part[:1024, :] + last[:1024, :]
    weights = part[1024:1025, :] + last[1024:1025, :]
    step_out[...], moment_out[...] = nesterov(total / weights, moment[...])


def nesterov(mean, moment):
    moment_new = 0.9 * moment + mean
    return 0.7 * (mean + 0.9 * moment_new), moment_new


def product(weight, tokens, start, upstream):
    part = tokens[:, pl.ds(pl.multiple_of(start, 256), 256)]
    return weight * lax.dot_general(part, upstream[...], (((0,), (0,)), ((), ())), preferred_element_type=F32)


def y_first_kernel(kinds):
    def body(at, weight, tokens, upstream, *outs):
        for kind, out in zip(kinds, outs):
            out[...] = product(weight, tokens, 1024 + 256 * place(at, kind, 2), upstream)

    return body


def x_first_kernel(at, weight, tokens, upstream, *refs):
    for y in range(4):
        grad = product(weight, tokens, 256 * y, upstream)
        for x in range(4):
            for kind, out in zip("ABCO", refs):

                @pl.when(place(at, kind, 3) == x)
                def _():
                    out[64 * y : 64 * y + 64, :] = grad[64 * x : 64 * x + 64, :]

    for out in refs:
        out[256:, :] = jnp.full((1, 1024), weight, F32)


def add_kernel(at, weight, a, b, out):
    out[...] = a[...] + b[...]


def add_two_kernel(at, weight, last, relayed, own, direct, last_out, own_out):
    last_out[...] = last[...] + relayed[...]
    own_out[...] = own[...] + direct[...]


def split_kernel(axis, extra):
    def body(at, weight, a, b, c, *outs):
        for kind, out in zip("ABCO", outs):
            rows = pl.ds(pl.multiple_of(64 * place(at, kind, axis), 64), 64)
            out[:64, :] = a[rows, :] + b[rows, :] + c[rows, :]
            if extra:
                out[64:, :] = a[256:, :] + b[256:, :] + c[256:, :]

    return body


def cross_kernel(at, weight, a, got_a, b, got_b, keep, other):
    first = a[...] + got_a[...]
    second = b[...] + got_b[...]
    low = at[4] == 0
    keep[:64, :] = jnp.where(low, first[:64, :], second)
    other[:64, :] = jnp.where(low, second, first[:64, :])
    keep[64:, :] = first[64:, :]
    other[64:, :] = first[64:, :]


def finish_one_kernel(at, weight, keep, got, moment, step_out, moment_out):
    total = keep[...] + got[...]
    step_out[...], moment_out[...] = nesterov(total[:64, :] / total[64:65, :], moment[...])


def on_device(counts, inputs, cotangent, delta_two, moment_one, moment_two):
    at = jnp.stack([lax.axis_index(n) for n in ("zhi", "core", "y", "x", "zlo")]).astype(jnp.int32)
    delta, tokens, upstream = delta_two[0, 0], inputs[0, 0], cotangent[0, 0]
    two, y_part, x_part = (1024 + EXTRA, 256), (256, 1024), (257, 1024)
    pair = (2 * two[0], 256)
    run = lambda body, name, shapes, *arrays, **more: call(body, name, shapes, at, counts, *arrays, **more)

    pair_ab = run(
        first_pair_kernel,
        "pair_ab",
        [pair],
        hbm=(delta,),
        scratch=[pltpu.VMEM((2, 1024, 256), jnp.bfloat16), pltpu.SemaphoreType.DMA((2,))],
    )
    got_ab = send(pair_ab, along("core", 1))
    ya = run(y_first_kernel("A"), "ya", [y_part], tokens, upstream, after=(pair_ab,))
    got_ya = send(ya, forward("y"))
    pair_co = run(pair_kernel, "pair_co", [pair], delta, after=(ya,))
    got_co = send(pair_co, along("core", 1))
    zab = run(z_first_kernel, "zab", [pair], delta, got_ab, after=(pair_co,))
    got_zab = send(zab, forward("zhi"))
    xa, xb, xc, xo = run(x_first_kernel, "x", [x_part] * 4, tokens, upstream, after=(zab,))
    got_xa, got_xb = send(xa, forward("x")), send(xb, backward("x"))
    yb = run(y_first_kernel("B"), "yb", [y_part], tokens, upstream, after=(xa, got_ya, got_co))
    got_yb = send(yb, backward("y"))
    yc, yo = run(y_first_kernel("CO"), "yco", [y_part] * 2, tokens, upstream, after=(yb,))
    xc = run(add_kernel, "xc", [x_part], xc, got_xa, after=(yc, got_xb))
    got_xc = send(xc, forward("x"))
    yc = run(add_kernel, "yc", [y_part], yc, got_ya, after=(xc, got_yb))
    got_yc = send(yc, forward("y"))
    zc, zo = run(z_last_kernel, "zc", [two] * 2, delta, got_co, got_zab, after=(yc,))
    got_zc = send(zc, lambda core: {"zhi": 1 if core == 0 else -1, "core": 1})

    a_part, b_part = (65, 1024), (64, 1024)
    aa, ab, ac, ao = run(split_kernel(2, True), "x_sum", [a_part] * 4, xo, got_xb, got_xc, after=(zc,))
    got_aa, got_ab = send(aa, forward("y")), send(ab, backward("y"))
    ba, bb, bc, bo = run(split_kernel(3, False), "y_sum", [b_part] * 4, yo, got_yb, got_yc, after=(aa,))
    got_ba, got_bb = send(ba, forward("x")), send(bb, backward("x"))
    ac, ao = run(add_two_kernel, "ac", [a_part] * 2, ac, got_aa, ao, got_ab, after=(ba,))
    got_ac = send(ac, forward("y"))
    bc, bo = run(add_two_kernel, "bc", [b_part] * 2, bc, got_ba, bo, got_bb, after=(ac,))
    got_bc = send(bc, forward("x"))
    keep, other = run(cross_kernel, "cross", [a_part] * 2, ao, got_ac, bo, got_bc)
    got = send(other, along("zlo", 1))
    step_one, moment_one_new = run(finish_one_kernel, "one", [(64, 1024)] * 2, keep, got, moment_one[0])
    step_two, moment_two_new = run(
        finish_two_kernel, "two", [(1024, 256)] * 2, zo, got_zc, moment_two[0], after=(step_one,)
    )
    return (step_one[None], moment_one_new[None], step_two[None], moment_two_new[None])


def solution(mesh):
    fine = Mesh(mesh.devices.reshape(SIZES), AXES)
    row, col = AXES[:3], AXES[3:]
    return jax.shard_map(
        on_device,
        mesh=fine,
        in_specs=(
            P(row, col),
            P(row, col, None, None),
            P(row, col, None, None),
            P(row, col, None, None),
            P(col, row, None),
            P(row, None, col),
        ),
        out_specs=(
            P(col, row, None),
            P(col, row, None),
            P(row, None, col),
            P(row, None, col),
        ),
        check_vma=False,
    )
```

```python
import jax
import jax.numpy as jnp
from jax import lax
from jax.experimental import pallas as pl
from jax.experimental.pallas import tpu as pltpu
from jax.sharding import Mesh, PartitionSpec as P

AXES = ("zlo", "y", "x", "zhi", "core")
SIZES = (2, 4, 4, 4, 2)
F32 = jnp.float32
EXTRA = 8


def permutation(shift):
    pairs = []
    for at in range(256):
        left, place = at, {}
        for name, size in zip(AXES[::-1], SIZES[::-1]):
            left, place[name] = divmod(left, size)
        step = shift(place["core"])
        to = 0
        for name, size in zip(AXES, SIZES):
            to = to * size + (place[name] + step.get(name, 0)) % size
        pairs.append((at, to))
    return pairs


def send(value, shift):
    return lax.ppermute(value, AXES, permutation(shift))


def forward(name):
    return lambda core: {name: 1 if core == 0 else -1}


def backward(name):
    return lambda core: {name: -1 if core == 0 else 1}


def along(name, step):
    return lambda core: {name: step}


def call(body, name, shapes, at, counts, *arrays, after=(), scratch=(), hbm=(), limit=24):
    n, held = len(arrays) + len(hbm), len(after)

    def kernel(at_ref, counts_ref, *refs):
        body(at_ref, counts_ref[0, 0].astype(F32), *refs[:n], *refs[n + held :])

    smem, vmem, hbm_, anywhere = (pl.BlockSpec(memory_space=s) for s in (pltpu.SMEM, pltpu.VMEM, pltpu.HBM, pl.ANY))
    out = pl.pallas_call(
        kernel,
        in_specs=[smem, smem] + [vmem] * len(arrays) + [hbm_] * len(hbm) + [anywhere] * held,
        out_specs=[vmem] * len(shapes),
        out_shape=[jax.ShapeDtypeStruct(s, F32) for s in shapes],
        scratch_shapes=scratch,
        compiler_params=pltpu.CompilerParams(vmem_limit_bytes=limit << 20),
        cost_estimate=pl.CostEstimate(flops=0, bytes_accessed=3 << 20, transcendentals=0),
        name=name,
    )(at, counts, *arrays, *hbm, *after)
    return out[0] if len(shapes) == 1 else out


def sign_of(at):
    return 1 - 2 * at[1]


def place(at, kind, axis):
    here = at[axis]
    return {"A": here + 2, "B": here + 4 - sign_of(at), "C": here + 4 + sign_of(at), "O": here}[kind] & 3


def column(at, kind, mine):
    core, sign = at[1], sign_of(at)
    if not mine:
        core, sign = 1 - core, -sign
    step, of = {"A": (2, 1 - core), "B": (sign, core), "C": (sign, 1 - core), "O": (0, core)}[kind]
    block = ((at[0] + 4 + step) & 3) * 2 + of
    return pl.ds(pl.multiple_of(block * 256, 256), 256)


ROWS = 1024 + EXTRA


def first_pair_kernel(at, weight, delta, out, blocks, sems):
    copies = [
        pltpu.make_async_copy(delta.at[:, column(at, kind, False)], blocks.at[i], sems.at[i])
        for i, kind in enumerate("AB")
    ]
    for copy in copies:
        copy.start()
    for i, copy in enumerate(copies):
        base = i * ROWS
        out[base + 1024 : base + ROWS, :] = jnp.full((EXTRA, 256), weight, F32)
        copy.wait()
        out[base : base + 1024, :] = weight * blocks[i].astype(F32)


def pair_kernel(at, weight, delta, *outs):
    for kind, out in zip("CO", outs):
        out[:1024, :] = weight * delta[:, column(at, kind, False)].astype(F32)
        out[1024:, :] = jnp.full((EXTRA, 256), weight, F32)


def add_block(out, to, at, weight, delta, kind, pair, base, got=None, got_base=0):
    total = weight * delta[:, column(at, kind, True)].astype(F32) + pair[base : base + 1024, :]
    weights = weight + pair[base + 1024 : base + ROWS, :]
    if got is not None:
        total += got[got_base : got_base + 1024, :]
        weights += got[got_base + 1024 : got_base + ROWS, :]
    out[to : to + 1024, :] = total
    out[to + 1024 : to + ROWS, :] = weights


SPLIT = 760


def z_first_kernel(at, weight, delta, pair, first, rest):
    add_block(first, 0, at, weight, delta, "A", pair, 0)
    total = weight * delta[:, column(at, "B", True)].astype(F32) + pair[ROWS : ROWS + 1024, :]
    first[ROWS : ROWS + SPLIT, :] = total[:SPLIT, :]
    first[ROWS + SPLIT :, :] = weight + pair[ROWS + 1024 :, :]
    rest[...] = total[SPLIT:, :]


def z_last_kernel(at, weight, delta, pair, got, last):
    add_block(last, 0, at, weight, delta, "C", pair, 0, got, 0)


def z_own_kernel(at, weight, delta, pair, got, rest, own):
    total = weight * delta[:, column(at, "O", True)].astype(F32) + pair[:1024, :]
    own[:SPLIT, :] = total[:SPLIT, :] + got[ROWS : ROWS + SPLIT, :]
    own[SPLIT:1024, :] = total[SPLIT:, :] + rest[...]
    own[1024:, :] = weight + pair[1024:, :] + got[ROWS + SPLIT :, :]


def finish_two_kernel(at, weight, part, last, moment, step_out, moment_out, done):
    total = part[:1024, :] + last[:1024, :]
    weights = part[1024:1025, :] + last[1024:1025, :]
    step_out[...], moment_out[...] = nesterov(total / weights, moment[...])
    done[...] = jnp.zeros((8, 128), F32)


def nesterov(mean, moment):
    moment_new = 0.9 * moment + mean
    return 0.7 * (mean + 0.9 * moment_new), moment_new


def product(weight, tokens, start, upstream):
    part = tokens[:, pl.ds(pl.multiple_of(start, 256), 256)]
    return weight * lax.dot_general(part, upstream[...], (((0,), (0,)), ((), ())), preferred_element_type=F32)


def y_first_kernel(kinds):
    def body(at, weight, tokens, upstream, *outs):
        for kind, out in zip(kinds, outs):
            out[:256, :] = product(weight, tokens, 1024 + 256 * place(at, kind, 2), upstream)
            out[256:, :] = jnp.full((1, 1024), weight, F32)

    return body


def x_first_kernel(at, weight, tokens, upstream, *refs):
    for y in range(4):
        grad = product(weight, tokens, 256 * y, upstream)
        for x in range(4):
            for kind, out in zip("ABCO", refs):

                @pl.when(place(at, kind, 3) == x)
                def _():
                    out[64 * y : 64 * y + 64, :] = grad[64 * x : 64 * x + 64, :]


def add_kernel(at, weight, a, b, out):
    out[...] = a[...] + b[...]


def add_two_kernel(at, weight, last, relayed, own, direct, last_out, own_out):
    last_out[...] = last[...] + relayed[...]
    own_out[...] = own[...] + direct[...]


def split_kernel(axis, extra):
    def body(at, weight, a, b, c, *outs):
        for kind, out in zip("ABCO", outs):
            rows = pl.ds(pl.multiple_of(64 * place(at, kind, axis), 64), 64)
            out[:64, :] = a[rows, :] + b[rows, :] + c[rows, :]
            if extra:
                out[64:, :] = a[256:, :] + b[256:, :] + c[256:, :]

    return body


def cross_kernel(at, weight, a, got_a, b, got_b, keep, other):
    first = a[...] + got_a[...]
    second = b[...] + got_b[...]
    low = at[4] == 0
    keep[:64, :] = jnp.where(low, first, second[:64, :])
    other[:64, :] = jnp.where(low, second[:64, :], first)
    keep[64:, :] = second[64:, :]
    other[64:, :] = second[64:, :]


def finish_one_kernel(at, weight, keep, got, moment, step_out, moment_out):
    total = keep[...] + got[...]
    step_out[...], moment_out[...] = nesterov(total[:64, :] / total[64:65, :], moment[...])


def on_device(counts, inputs, cotangent, delta_two, moment_one, moment_two):
    at = jnp.stack([lax.axis_index(n) for n in ("zhi", "core", "y", "x", "zlo")]).astype(jnp.int32)
    delta, tokens, upstream = delta_two[0, 0], inputs[0, 0], cotangent[0, 0]
    two, y_part, x_part = (1024 + EXTRA, 256), (257, 1024), (256, 1024)
    pair = (2 * two[0], 256)
    run = lambda body, name, shapes, *arrays, **more: call(body, name, shapes, at, counts, *arrays, **more)

    pair_ab = run(
        first_pair_kernel,
        "pair_ab",
        [pair],
        hbm=(delta,),
        scratch=[pltpu.VMEM((2, 1024, 256), jnp.bfloat16), pltpu.SemaphoreType.DMA((2,))],
        limit=49,
    )
    got_ab = send(pair_ab, along("core", 1))
    ya, yb = run(y_first_kernel("AB"), "yab", [y_part] * 2, tokens, upstream, after=(pair_ab,))
    got_ya, got_yb = send(ya, forward("y")), send(yb, backward("y"))
    za, zb = run(
        z_first_kernel, "zab", [(ROWS + SPLIT + EXTRA, 256), (1024 - SPLIT, 256)], delta, got_ab, after=(ya,)
    )
    got_za, got_zb = send(za, forward("zhi")), send(zb, forward("zhi"))
    xa, xb, xc, xo = run(x_first_kernel, "x", [x_part] * 4, tokens, upstream, after=(za,))
    got_xa, got_xb = send(xa, forward("x")), send(xb, backward("x"))
    yc, yo = run(y_first_kernel("CO"), "yco", [y_part] * 2, tokens, upstream, after=(xa,))
    pair_c, pair_o = run(pair_kernel, "pair_co", [two] * 2, delta, after=(yc,))
    got_c, got_o = send(pair_c, along("core", 1)), send(pair_o, along("core", 1))
    yc = run(add_kernel, "yc", [y_part], yc, got_ya, after=(got_yb, pair_o))
    got_yc = send(yc, forward("y"))
    xc = run(add_kernel, "xc", [x_part], xc, got_xa, after=(yc, got_xb))
    got_xc = send(xc, forward("x"))
    zc = run(z_last_kernel, "zc", [two], delta, got_c, got_za, after=(xc,))
    got_zc = send(zc, lambda core: {"zhi": 1 if core == 0 else -1, "core": 1})

    a_part, b_part = (64, 1024), (65, 1024)
    ba, bb, bc, bo = run(split_kernel(3, True), "y_sum", [b_part] * 4, yo, got_yb, got_yc, after=(zc,))
    got_ba, got_bb = send(ba, forward("x")), send(bb, backward("x"))
    zo = run(z_own_kernel, "zo", [two], delta, got_o, got_za, got_zb, after=(ba,))
    aa, ab, ac, ao = run(split_kernel(2, False), "x_sum", [a_part] * 4, xo, got_xb, got_xc, after=(zo,))
    got_aa, got_ab = send(aa, forward("y")), send(ab, backward("y"))
    bc, bo = run(add_two_kernel, "bc", [b_part] * 2, bc, got_ba, bo, got_bb, after=(aa,))
    got_bc = send(bc, forward("x"))
    ac, ao = run(add_two_kernel, "ac", [a_part] * 2, ac, got_aa, ao, got_ab, after=(bc,))
    got_ac = send(ac, forward("y"))
    keep, other = run(cross_kernel, "cross", [b_part] * 2, ao, got_ac, bo, got_bc)
    got = send(other, along("zlo", 1))
    step_two, moment_two_new, done = run(
        finish_two_kernel, "two", [(1024, 256)] * 2 + [(8, 128)], zo, got_zc, moment_two[0], after=(keep,)
    )
    step_one, moment_one_new = run(
        finish_one_kernel, "one", [(64, 1024)] * 2, keep, got, moment_one[0], after=(done,)
    )
    return (step_one[None], moment_one_new[None], step_two[None], moment_two_new[None])


def solution(mesh):
    fine = Mesh(mesh.devices.reshape(SIZES), AXES)
    row, col = AXES[:3], AXES[3:]
    return jax.shard_map(
        on_device,
        mesh=fine,
        in_specs=(
            P(row, col),
            P(row, col, None, None),
            P(row, col, None, None),
            P(row, col, None, None),
            P(col, row, None),
            P(row, None, col),
        ),
        out_specs=(
            P(col, row, None),
            P(col, row, None),
            P(row, None, col),
            P(row, None, col),
        ),
        check_vma=False,
    )
```

```python
import jax
import jax.numpy as jnp
from jax import lax
from jax.experimental import pallas as pl
from jax.experimental.pallas import tpu as pltpu
from jax.sharding import Mesh, PartitionSpec as P

AXES = ("zlo", "y", "x", "zhi", "core")
SIZES = (2, 4, 4, 4, 2)
F32 = jnp.float32
EXTRA = 8


def permutation(shift):
    pairs = []
    for at in range(256):
        left, place = at, {}
        for name, size in zip(AXES[::-1], SIZES[::-1]):
            left, place[name] = divmod(left, size)
        step = shift(place["core"])
        to = 0
        for name, size in zip(AXES, SIZES):
            to = to * size + (place[name] + step.get(name, 0)) % size
        pairs.append((at, to))
    return pairs


def send(value, shift):
    return lax.ppermute(value, AXES, permutation(shift))


def forward(name):
    return lambda core: {name: 1 if core == 0 else -1}


def backward(name):
    return lambda core: {name: -1 if core == 0 else 1}


def along(name, step):
    return lambda core: {name: step}


def call(body, name, shapes, counts, *arrays, after=(), scratch=(), hbm=(), hbm_outs=0, limit=24):
    n, held = len(arrays) + len(hbm), len(after)

    def kernel(counts_ref, *refs):
        at = [lax.axis_index(name) for name in ("zhi", "core", "y", "x", "zlo")]
        body(at, counts_ref[0, 0].astype(F32), *refs[:n], *refs[n + held :])

    smem, vmem, hbm_, anywhere = (pl.BlockSpec(memory_space=s) for s in (pltpu.SMEM, pltpu.VMEM, pltpu.HBM, pl.ANY))
    out = pl.pallas_call(
        kernel,
        in_specs=[smem] + [vmem] * len(arrays) + [hbm_] * len(hbm) + [anywhere] * held,
        out_specs=[anywhere] * hbm_outs + [vmem] * (len(shapes) - hbm_outs),
        out_shape=[jax.ShapeDtypeStruct(s, F32) for s in shapes],
        scratch_shapes=scratch,
        compiler_params=pltpu.CompilerParams(vmem_limit_bytes=limit << 20),
        cost_estimate=pl.CostEstimate(flops=0, bytes_accessed=3 << 20, transcendentals=0),
        name=name,
    )(counts, *arrays, *hbm, *after)
    return out[0] if len(shapes) == 1 else out


def sign_of(at):
    return 1 - 2 * at[1]


def place(at, kind, axis):
    here = at[axis]
    return {"A": here + 2, "B": here + 4 - sign_of(at), "C": here + 4 + sign_of(at), "O": here}[kind] & 3


def column(at, kind, mine):
    core, sign = at[1], sign_of(at)
    if not mine:
        core, sign = 1 - core, -sign
    step, of = {"A": (2, 1 - core), "B": (sign, core), "C": (sign, 1 - core), "O": (0, core)}[kind]
    block = ((at[0] + 4 + step) & 3) * 2 + of
    return pl.ds(pl.multiple_of(block * 256, 256), 256)


ROWS = 1024 + EXTRA


SPLIT = 768
FIRST = ROWS + SPLIT + EXTRA


def first_pair_kernel(at, weight, delta, out, first, second, sems):
    copies = [
        pltpu.make_async_copy(delta.at[:, column(at, "A", False)], first, sems.at[0]),
        pltpu.make_async_copy(delta.at[:SPLIT, column(at, "B", False)], second, sems.at[1]),
    ]
    for copy in copies:
        copy.start()
    out[1024:ROWS, :] = jnp.full((EXTRA, 256), weight, F32)
    out[ROWS + SPLIT :, :] = jnp.full((EXTRA, 256), weight, F32)
    copies[0].wait()
    out[:1024, :] = weight * first[...].astype(F32)
    copies[1].wait()
    out[ROWS : ROWS + SPLIT, :] = weight * second[...].astype(F32)


def pair_kernel(at, weight, delta, last, own):
    for kind, out in (("C", last), ("O", own)):
        out[:1024, :] = weight * delta[:, column(at, kind, False)].astype(F32)
        out[1024:ROWS, :] = jnp.full((EXTRA, 256), weight, F32)
    last[ROWS:, :] = weight * delta[SPLIT:, column(at, "B", False)].astype(F32)


def add_block(out, to, at, weight, delta, kind, pair, base, got=None, got_base=0):
    total = weight * delta[:, column(at, kind, True)].astype(F32) + pair[base : base + 1024, :]
    weights = weight + pair[base + 1024 : base + ROWS, :]
    if got is not None:
        total += got[got_base : got_base + 1024, :]
        weights += got[got_base + 1024 : got_base + ROWS, :]
    out[to : to + 1024, :] = total
    out[to + 1024 : to + ROWS, :] = weights


def z_first_kernel(at, weight, delta, pair, first):
    add_block(first, 0, at, weight, delta, "A", pair, 0)
    total = weight * delta[:SPLIT, column(at, "B", True)].astype(F32) + pair[ROWS : ROWS + SPLIT, :]
    first[ROWS : ROWS + SPLIT, :] = total
    first[ROWS + SPLIT :, :] = weight + pair[ROWS + SPLIT : ROWS + SPLIT + 4, :]


def z_rest_kernel(at, weight, delta, pair, rest):
    rest[...] = weight * delta[SPLIT:, column(at, "B", True)].astype(F32) + pair[ROWS:, :]


def z_last_kernel(at, weight, delta, pair, got, last):
    add_block(last, 0, at, weight, delta, "C", pair, 0, got, 0)


def z_own_kernel(at, weight, delta, pair, got, rest, own):
    total = weight * delta[:, column(at, "O", True)].astype(F32) + pair[:1024, :]
    own[:SPLIT, :] = total[:SPLIT, :] + got[ROWS : ROWS + SPLIT, :]
    own[SPLIT:1024, :] = total[SPLIT:, :] + rest[...]
    own[1024:1028, :] = weight + pair[1024:1028, :] + got[ROWS + SPLIT :, :]
    own[1028:, :] = jnp.zeros((4, 256), F32)


def finish(parts, rows, mean, moment, outs, stores, sems):
    copies = []
    for i in range(parts):
        part = slice(i * rows, (i + 1) * rows)
        here = mean(part)
        new = 0.9 * moment[part, :] + here
        stores[0][part, :] = 0.7 * (here + 0.9 * new)
        stores[1][part, :] = new
        for k in range(2):
            copy = pltpu.make_async_copy(stores[k].at[part, :], outs[k].at[part, :], sems.at[k, i])
            copy.start()
            copies.append(copy)
    for copy in copies:
        copy.wait()


def finish_two_kernel(at, weight, part, last, moment, step_out, moment_out, done, *scratch):
    weights = part[1024:1025, :] + last[1024:1025, :]
    mean = lambda rows: (part[rows, :] + last[rows, :]) / weights
    finish(4, 256, mean, moment, (step_out, moment_out), scratch[:2], scratch[2])
    done[...] = jnp.zeros((8, 128), F32)


def product(weight, tokens, start, upstream):
    part = tokens[:, pl.ds(pl.multiple_of(start, 256), 256)]
    return weight * lax.dot_general(part, upstream[...], (((0,), (0,)), ((), ())), preferred_element_type=F32)


def y_first_kernel(kinds):
    def body(at, weight, tokens, upstream, *outs):
        for kind, out in zip(kinds, outs):
            out[:256, :] = product(weight, tokens, 1024 * (1 - at[4]) + 256 * place(at, kind, 2), upstream)
            out[256:, :] = jnp.full((1, 1024), weight, F32)

    return body


def x_first_kernel(at, weight, tokens, upstream, *refs):
    for y in range(4):
        grad = product(weight, tokens, 1024 * at[4] + 256 * y, upstream)
        for x in range(4):
            for kind, out in zip("ABCO", refs):

                @pl.when(place(at, kind, 3) == x)
                def _():
                    out[64 * y : 64 * y + 64, :] = grad[64 * x : 64 * x + 64, :]


def add_kernel(at, weight, a, b, out):
    out[...] = a[...] + b[...]


def add_two_kernel(at, weight, last, relayed, own, direct, last_out, own_out):
    last_out[...] = last[...] + relayed[...]
    own_out[...] = own[...] + direct[...]


def flat(tail):
    return (8, 8 * 1024 + 128 * tail)


def split_kernel(axis, extra):
    def body(at, weight, a, b, c, *outs):
        for kind, out in zip("ABCO", outs):
            rows = pl.ds(pl.multiple_of(64 * place(at, kind, axis), 64), 64)
            total = a[rows, :] + b[rows, :] + c[rows, :]
            for i in range(8):
                out[:, 1024 * i : 1024 * i + 1024] = total[8 * i : 8 * i + 8, :]
            shape = (8, out.shape[1] - 8192)
            if extra:
                weights = a[256:257, :128] + b[256:257, :128] + c[256:257, :128]
                out[:, 8192:] = jnp.broadcast_to(weights, shape)
            else:
                out[:, 8192:] = jnp.zeros(shape, F32)

    return body


def finish_one_kernel(at, weight, own, last, other, got, moment, step_out, moment_out, *scratch):
    weights = jnp.concatenate([other[:, 8192:] + got[:, 8192:]] * 8, axis=1)

    def mean(rows):
        groups = [slice(128 * i, 128 * i + 1024) for i in range(rows.start, rows.stop, 8)]
        return jnp.concatenate([(own[:, g] + last[:, g] + got[:, g]) / weights for g in groups], axis=0)

    finish(2, 32, mean, moment, (step_out, moment_out), scratch[:2], scratch[2])


def on_device(counts, inputs, cotangent, delta_two, moment_one, moment_two):
    delta, tokens, upstream = delta_two[0, 0], inputs[0, 0], cotangent[0, 0]
    two, y_part, x_part = (1024 + EXTRA, 256), (257, 1024), (256, 1024)
    run = lambda body, name, shapes, *arrays, **more: call(body, name, shapes, counts, *arrays, **more)

    pair_ab = run(
        first_pair_kernel,
        "pair_ab",
        [(FIRST, 256)],
        hbm=(delta,),
        scratch=[pltpu.VMEM((rows, 256), jnp.bfloat16) for rows in (1024, SPLIT)] + [pltpu.SemaphoreType.DMA((2,))],
        limit=49,
    )
    got_ab = send(pair_ab, along("core", 1))
    ya, yb = run(y_first_kernel("AB"), "yab", [y_part] * 2, tokens, upstream, after=(pair_ab,))
    got_ya, got_yb = send(ya, forward("y")), send(yb, backward("y"))
    za = run(z_first_kernel, "zab", [(ROWS + SPLIT + 4, 256)], delta, got_ab, after=(ya,))
    got_za = send(za, forward("zhi"))
    xa, xb, xc, xo = run(x_first_kernel, "x", [x_part] * 4, tokens, upstream, after=(za,))
    got_xa, got_xb = send(xa, forward("x")), send(xb, backward("x"))
    yc, yo = run(y_first_kernel("CO"), "yco", [y_part] * 2, tokens, upstream, after=(xa,))
    pair_c, pair_o = run(pair_kernel, "pair_co", [(two[0] + 1024 - SPLIT, 256), two], delta, after=(yc,))
    got_c, got_o = send(pair_c, along("core", 1)), send(pair_o, along("core", 1))
    yc = run(add_kernel, "yc", [y_part], yc, got_ya, after=(got_yb, pair_o))
    got_yc = send(yc, forward("y"))
    xc = run(add_kernel, "xc", [x_part], xc, got_xa, after=(yc, got_xb))
    got_xc = send(xc, forward("x"))
    zb = run(z_rest_kernel, "zb", [(1024 - SPLIT, 256)], delta, got_c, after=(xc,))
    got_zb = send(zb, forward("zhi"))
    zc = run(z_last_kernel, "zc", [two], delta, got_c, got_za, after=(zb,))
    got_zc = send(zc, lambda core: {"zhi": 1 if core == 0 else -1, "core": 1})
    zo = run(z_own_kernel, "zo", [two], delta, got_o, got_za, got_zb, after=(zc,))

    a_part, b_part = flat(2), flat(1)
    ba, bb, bc, bo = run(split_kernel(3, True), "y_sum", [b_part] * 4, yo, got_yb, got_yc, after=(zo,))
    got_ba, got_bb = send(ba, forward("x")), send(bb, backward("x"))
    aa, ab, ac, ao = run(split_kernel(2, False), "x_sum", [a_part] * 4, xo, got_xb, got_xc, after=(ba,))
    got_aa, got_ab = send(aa, forward("y")), send(ab, backward("y"))
    bc, bo = run(add_two_kernel, "bc", [b_part] * 2, bc, got_ba, bo, got_bb, after=(aa,))
    got_bc = send(bc, forward("x"))
    ac, ao = run(add_two_kernel, "ac", [a_part] * 2, ac, got_aa, ao, got_ab, after=(bc,))
    got_ac = send(ac, forward("y"))
    other = run(add_kernel, "cross", [b_part], bo, got_bc, after=(ac,))
    got = send(other, along("zlo", 1))
    step_two, moment_two_new, done = run(
        finish_two_kernel, "two", [(1024, 256)] * 2 + [(8, 128)], zo, got_zc, moment_two[0], after=(other,), hbm_outs=2,
        scratch=[pltpu.VMEM((1024, 256), F32)] * 2 + [pltpu.SemaphoreType.DMA((2, 4))],
    )
    step_one, moment_one_new = run(
        finish_one_kernel, "one", [(64, 1024)] * 2, ao, got_ac, other, got, moment_one[0], after=(done,), hbm_outs=2,
        scratch=[pltpu.VMEM((64, 1024), F32)] * 2 + [pltpu.SemaphoreType.DMA((2, 2))],
    )
    return (step_one[None], moment_one_new[None], step_two[None], moment_two_new[None])


def solution(mesh):
    fine = Mesh(mesh.devices.reshape(SIZES), AXES)
    row, col = AXES[:3], AXES[3:]
    return jax.shard_map(
        on_device,
        mesh=fine,
        in_specs=(
            P(row, col),
            P(row, col, None, None),
            P(row, col, None, None),
            P(row, col, None, None),
            P(col, row, None),
            P(row, None, col),
        ),
        out_specs=(
            P(col, row, None),
            P(col, row, None),
            P(row, None, col),
            P(row, None, col),
        ),
        check_vma=False,
    )
```

```python
import jax
import jax.numpy as jnp
from jax import lax
from jax.experimental import pallas as pl
from jax.experimental.pallas import tpu as pltpu
from jax.sharding import Mesh, PartitionSpec as P

AXES = ("zlo", "y", "x", "zhi", "core")
SIZES = (2, 4, 4, 4, 2)
F32 = jnp.float32
EXTRA = 8


def permutation(shift):
    pairs = []
    for at in range(256):
        left, place = at, {}
        for name, size in zip(AXES[::-1], SIZES[::-1]):
            left, place[name] = divmod(left, size)
        step = shift(place["core"])
        to = 0
        for name, size in zip(AXES, SIZES):
            to = to * size + (place[name] + step.get(name, 0)) % size
        pairs.append((at, to))
    return pairs


def send(value, shift):
    return lax.ppermute(value, AXES, permutation(shift))


def forward(name):
    return lambda core: {name: 1 if core == 0 else -1}


def backward(name):
    return lambda core: {name: -1 if core == 0 else 1}


def along(name, step):
    return lambda core: {name: step}


def call(body, name, shapes, counts, *arrays, after=(), scratch=(), hbm=(), hbm_outs=0, limit=24):
    n, held = len(arrays) + len(hbm), len(after)

    def kernel(counts_ref, *refs):
        at = [lax.axis_index(name) for name in ("zhi", "core", "y", "x", "zlo")]
        body(at, counts_ref[0, 0].astype(F32), *refs[:n], *refs[n + held :])

    smem, vmem, hbm_, anywhere = (pl.BlockSpec(memory_space=s) for s in (pltpu.SMEM, pltpu.VMEM, pltpu.HBM, pl.ANY))
    out = pl.pallas_call(
        kernel,
        in_specs=[smem] + [vmem] * len(arrays) + [hbm_] * len(hbm) + [anywhere] * held,
        out_specs=[anywhere] * hbm_outs + [vmem] * (len(shapes) - hbm_outs),
        out_shape=[jax.ShapeDtypeStruct(s, F32) for s in shapes],
        scratch_shapes=scratch,
        compiler_params=pltpu.CompilerParams(vmem_limit_bytes=limit << 20),
        cost_estimate=pl.CostEstimate(flops=0, bytes_accessed=3 << 20, transcendentals=0),
        name=name,
    )(counts, *arrays, *hbm, *after)
    return out[0] if len(shapes) == 1 else out


def sign_of(at):
    return 1 - 2 * at[1]


def place(at, kind, axis):
    here = at[axis]
    return {"A": here + 2, "B": here + 4 - sign_of(at), "C": here + 4 + sign_of(at), "O": here}[kind] & 3


def column(at, kind, mine):
    core, sign = at[1], sign_of(at)
    if not mine:
        core, sign = 1 - core, -sign
    step, of = {"A": (2, 1 - core), "B": (sign, core), "C": (sign, 1 - core), "O": (0, core)}[kind]
    block = ((at[0] + 4 + step) & 3) * 2 + of
    return pl.ds(pl.multiple_of(block * 256, 256), 256)


ROWS = 1024 + EXTRA


SPLIT = 768
FIRST = ROWS + SPLIT + EXTRA


def first_pair_kernel(at, weight, delta, out, first, second, sems):
    copies = [
        pltpu.make_async_copy(delta.at[:, column(at, "A", False)], first, sems.at[0]),
        pltpu.make_async_copy(delta.at[:SPLIT, column(at, "B", False)], second, sems.at[1]),
    ]
    for copy in copies:
        copy.start()
    out[1024:ROWS, :] = jnp.full((EXTRA, 256), weight, F32)
    out[ROWS + SPLIT :, :] = jnp.full((EXTRA, 256), weight, F32)
    copies[0].wait()
    out[:1024, :] = weight * first[...].astype(F32)
    copies[1].wait()
    out[ROWS : ROWS + SPLIT, :] = weight * second[...].astype(F32)


def pair_kernel(at, weight, delta, last, own):
    for kind, out in (("C", last), ("O", own)):
        out[:1024, :] = weight * delta[:, column(at, kind, False)].astype(F32)
        out[1024:ROWS, :] = jnp.full((EXTRA, 256), weight, F32)
    last[ROWS:, :] = weight * delta[SPLIT:, column(at, "B", False)].astype(F32)


def add_block(out, to, at, weight, delta, kind, pair, base, got=None, got_base=0):
    total = weight * delta[:, column(at, kind, True)].astype(F32) + pair[base : base + 1024, :]
    weights = weight + pair[base + 1024 : base + ROWS, :]
    if got is not None:
        total += got[got_base : got_base + 1024, :]
        weights += got[got_base + 1024 : got_base + ROWS, :]
    out[to : to + 1024, :] = total
    out[to + 1024 : to + ROWS, :] = weights


def z_first_kernel(at, weight, delta, pair, first):
    add_block(first, 0, at, weight, delta, "A", pair, 0)
    total = weight * delta[:SPLIT, column(at, "B", True)].astype(F32) + pair[ROWS : ROWS + SPLIT, :]
    first[ROWS : ROWS + SPLIT, :] = total
    first[ROWS + SPLIT :, :] = weight + pair[ROWS + SPLIT : ROWS + SPLIT + 4, :]


def z_rest_kernel(at, weight, delta, pair, rest):
    rest[...] = weight * delta[SPLIT:, column(at, "B", True)].astype(F32) + pair[ROWS:, :]


def z_last_kernel(at, weight, delta, pair, got, last):
    add_block(last, 0, at, weight, delta, "C", pair, 0, got, 0)


def z_own_kernel(at, weight, delta, pair, got, rest, own):
    total = weight * delta[:, column(at, "O", True)].astype(F32) + pair[:1024, :]
    own[:SPLIT, :] = total[:SPLIT, :] + got[ROWS : ROWS + SPLIT, :]
    own[SPLIT:1024, :] = total[SPLIT:, :] + rest[...]
    own[1024:1028, :] = weight + pair[1024:1028, :] + got[ROWS + SPLIT :, :]
    own[1028:, :] = jnp.zeros((4, 256), F32)


def finish(parts, rows, mean, moment, outs, stores, sems):
    copies = []
    for i in range(parts):
        part = slice(i * rows, (i + 1) * rows)
        here = mean(part)
        new = 0.9 * moment[part, :] + here
        stores[0][part, :] = 0.7 * (here + 0.9 * new)
        stores[1][part, :] = new
        for k in range(2):
            copy = pltpu.make_async_copy(stores[k].at[part, :], outs[k].at[part, :], sems.at[k, i])
            copy.start()
            copies.append(copy)
    return copies


def finish_kernel(at, weight, part, last_two, moment_two, own, last, other, got, moment_one, *refs):
    outs_one, outs_two, stores_one, stores_two = refs[:2], refs[2:4], refs[4:6], refs[6:8]
    weights_two = part[1024:1025, :] + last_two[1024:1025, :]
    weights_one = jnp.concatenate([other[:, 8192:] + got[:, 8192:]] * 8, axis=1)

    def mean_two(rows):
        return (part[rows, :] + last_two[rows, :]) / weights_two

    def mean_one(rows):
        groups = [slice(128 * i, 128 * i + 1024) for i in range(rows.start, rows.stop, 8)]
        return jnp.concatenate([(own[:, g] + last[:, g] + got[:, g]) / weights_one for g in groups], axis=0)

    copies = finish(4, 256, mean_two, moment_two, outs_two, stores_two, refs[8])
    copies += finish(1, 64, mean_one, moment_one, outs_one, stores_one, refs[9])
    for copy in copies:
        copy.wait()


def product(weight, tokens, start, upstream):
    part = tokens[:, pl.ds(pl.multiple_of(start, 256), 256)]
    return weight * lax.dot_general(part, upstream[...], (((0,), (0,)), ((), ())), preferred_element_type=F32)


def y_first_kernel(kinds):
    def body(at, weight, tokens, upstream, *outs):
        for kind, out in zip(kinds, outs):
            out[:256, :] = product(weight, tokens, 1024 * (1 - at[4]) + 256 * place(at, kind, 2), upstream)
            out[256:, :] = jnp.full((1, 1024), weight, F32)

    return body


def x_first_kernel(at, weight, tokens, upstream, *refs):
    for y in range(4):
        grad = product(weight, tokens, 1024 * at[4] + 256 * y, upstream)
        for x in range(4):
            for kind, out in zip("ABCO", refs):

                @pl.when(place(at, kind, 3) == x)
                def _():
                    out[64 * y : 64 * y + 64, :] = grad[64 * x : 64 * x + 64, :]


def add_kernel(at, weight, a, b, out):
    out[...] = a[...] + b[...]


def add_two_kernel(at, weight, last, relayed, own, direct, last_out, own_out):
    last_out[...] = last[...] + relayed[...]
    own_out[...] = own[...] + direct[...]


def flat(tail):
    return (8, 8 * 1024 + 128 * tail)


def split_kernel(axis, extra):
    def body(at, weight, a, b, c, *outs):
        for kind, out in zip("ABCO", outs):
            rows = pl.ds(pl.multiple_of(64 * place(at, kind, axis), 64), 64)
            total = a[rows, :] + b[rows, :] + c[rows, :]
            for i in range(8):
                out[:, 1024 * i : 1024 * i + 1024] = total[8 * i : 8 * i + 8, :]
            shape = (8, out.shape[1] - 8192)
            if extra:
                weights = a[256:257, :128] + b[256:257, :128] + c[256:257, :128]
                out[:, 8192:] = jnp.broadcast_to(weights, shape)
            else:
                out[:, 8192:] = jnp.zeros(shape, F32)

    return body


def on_device(counts, inputs, cotangent, delta_two, moment_one, moment_two):
    delta, tokens, upstream = delta_two[0, 0], inputs[0, 0], cotangent[0, 0]
    two, y_part, x_part = (1024 + EXTRA, 256), (257, 1024), (256, 1024)
    run = lambda body, name, shapes, *arrays, **more: call(body, name, shapes, counts, *arrays, **more)

    pair_ab = run(
        first_pair_kernel,
        "pair_ab",
        [(FIRST, 256)],
        hbm=(delta,),
        scratch=[pltpu.VMEM((rows, 256), jnp.bfloat16) for rows in (1024, SPLIT)] + [pltpu.SemaphoreType.DMA((2,))],
        limit=49,
    )
    got_ab = send(pair_ab, along("core", 1))
    ya, yb = run(y_first_kernel("AB"), "yab", [y_part] * 2, tokens, upstream, after=(pair_ab,))
    got_ya, got_yb = send(ya, forward("y")), send(yb, backward("y"))
    za = run(z_first_kernel, "zab", [(ROWS + SPLIT + 4, 256)], delta, got_ab, after=(ya,))
    got_za = send(za, forward("zhi"))
    xa, xb, xc, xo = run(x_first_kernel, "x", [x_part] * 4, tokens, upstream, after=(za,))
    got_xa, got_xb = send(xa, forward("x")), send(xb, backward("x"))
    yc, yo = run(y_first_kernel("CO"), "yco", [y_part] * 2, tokens, upstream, after=(xa,))
    pair_c, pair_o = run(pair_kernel, "pair_co", [(two[0] + 1024 - SPLIT, 256), two], delta, after=(yc,))
    got_c, got_o = send(pair_c, along("core", 1)), send(pair_o, along("core", 1))
    yc = run(add_kernel, "yc", [y_part], yc, got_ya, after=(got_yb, pair_o))
    got_yc = send(yc, forward("y"))
    xc = run(add_kernel, "xc", [x_part], xc, got_xa, after=(yc, got_xb))
    got_xc = send(xc, forward("x"))
    zb = run(z_rest_kernel, "zb", [(1024 - SPLIT, 256)], delta, got_c, after=(xc,))
    got_zb = send(zb, forward("zhi"))
    zc = run(z_last_kernel, "zc", [two], delta, got_c, got_za, after=(zb,))
    got_zc = send(zc, lambda core: {"zhi": 1 if core == 0 else -1, "core": 1})
    zo = run(z_own_kernel, "zo", [two], delta, got_o, got_za, got_zb, after=(zc,))

    a_part, b_part = flat(2), flat(1)
    ba, bb, bc, bo = run(split_kernel(3, True), "y_sum", [b_part] * 4, yo, got_yb, got_yc, after=(zo,))
    got_ba, got_bb = send(ba, forward("x")), send(bb, backward("x"))
    aa, ab, ac, ao = run(split_kernel(2, False), "x_sum", [a_part] * 4, xo, got_xb, got_xc, after=(ba,))
    got_aa, got_ab = send(aa, forward("y")), send(ab, backward("y"))
    bc, bo = run(add_two_kernel, "bc", [b_part] * 2, bc, got_ba, bo, got_bb, after=(aa,))
    got_bc = send(bc, forward("x"))
    ac, ao = run(add_two_kernel, "ac", [a_part] * 2, ac, got_aa, ao, got_ab, after=(bc,))
    got_ac = send(ac, forward("y"))
    other = run(add_kernel, "cross", [b_part], bo, got_bc, after=(ac,))
    got = send(other, along("zlo", 1))
    step_one, moment_one_new, step_two, moment_two_new = run(
        finish_kernel,
        "finish",
        [(64, 1024)] * 2 + [(1024, 256)] * 2,
        *(zo, got_zc, moment_two[0], ao, got_ac, other, got, moment_one[0]),
        hbm_outs=4,
        scratch=[pltpu.VMEM((64, 1024), F32)] * 2
        + [pltpu.VMEM((1024, 256), F32)] * 2
        + [pltpu.SemaphoreType.DMA((2, 4)), pltpu.SemaphoreType.DMA((2, 1))],
    )
    return (step_one[None], moment_one_new[None], step_two[None], moment_two_new[None])


def solution(mesh):
    fine = Mesh(mesh.devices.reshape(SIZES), AXES)
    row, col = AXES[:3], AXES[3:]
    return jax.shard_map(
        on_device,
        mesh=fine,
        in_specs=(
            P(row, col),
            P(row, col, None, None),
            P(row, col, None, None),
            P(row, col, None, None),
            P(col, row, None),
            P(row, None, col),
        ),
        out_specs=(
            P(col, row, None),
            P(col, row, None),
            P(row, None, col),
            P(row, None, col),
        ),
        check_vma=False,
    )
```

```python
import jax
import jax.numpy as jnp
from jax import lax
from jax.experimental import pallas as pl
from jax.experimental.pallas import tpu as pltpu
from jax.sharding import Mesh, PartitionSpec as P

AXES = ("zlo", "y", "x", "zhi", "core")
SIZES = (2, 4, 4, 4, 2)
F32 = jnp.float32
EXTRA = 8


def permutation(shift):
    pairs = []
    for at in range(256):
        left, place = at, {}
        for name, size in zip(AXES[::-1], SIZES[::-1]):
            left, place[name] = divmod(left, size)
        step = shift(place["core"])
        to = 0
        for name, size in zip(AXES, SIZES):
            to = to * size + (place[name] + step.get(name, 0)) % size
        pairs.append((at, to))
    return pairs


def send(value, shift):
    return lax.ppermute(value, AXES, permutation(shift))


def forward(name):
    return lambda core: {name: 1 if core == 0 else -1}


def backward(name):
    return lambda core: {name: -1 if core == 0 else 1}


def along(name, step):
    return lambda core: {name: step}


def call(body, name, shapes, counts, *arrays, after=(), scratch=(), hbm=(), hbm_outs=0, limit=24):
    n, held = len(arrays) + len(hbm), len(after)

    def kernel(counts_ref, *refs):
        at = [lax.axis_index(name) for name in ("zhi", "core", "y", "x", "zlo")]
        body(at, counts_ref[0, 0].astype(F32), *refs[:n], *refs[n + held :])

    smem, vmem, hbm_, anywhere = (pl.BlockSpec(memory_space=s) for s in (pltpu.SMEM, pltpu.VMEM, pltpu.HBM, pl.ANY))
    out = pl.pallas_call(
        kernel,
        in_specs=[smem] + [vmem] * len(arrays) + [hbm_] * len(hbm) + [anywhere] * held,
        out_specs=[anywhere] * hbm_outs + [vmem] * (len(shapes) - hbm_outs),
        out_shape=[jax.ShapeDtypeStruct(s, F32) for s in shapes],
        scratch_shapes=scratch,
        compiler_params=pltpu.CompilerParams(vmem_limit_bytes=limit << 20),
        cost_estimate=pl.CostEstimate(flops=0, bytes_accessed=3 << 20, transcendentals=0),
        name=name,
    )(counts, *arrays, *hbm, *after)
    return out[0] if len(shapes) == 1 else out


def sign_of(at):
    return 1 - 2 * at[1]


def place(at, kind, axis):
    here = at[axis]
    return {"A": here + 2, "B": here + 4 - sign_of(at), "C": here + 4 + sign_of(at), "O": here}[kind] & 3


def column(at, kind, mine):
    core, sign = at[1], sign_of(at)
    if not mine:
        core, sign = 1 - core, -sign
    step, of = {"A": (2, 1 - core), "B": (sign, core), "C": (sign, 1 - core), "O": (0, core)}[kind]
    block = ((at[0] + 4 + step) & 3) * 2 + of
    return pl.ds(pl.multiple_of(block * 256, 256), 256)


ROWS = 1024 + EXTRA


SPLIT = 776
FIRST = 1024 + SPLIT + EXTRA
REST = 768
READ = 784


def first_pair_kernel(at, weight, delta, out, first, second, sems):
    copies = [
        pltpu.make_async_copy(delta.at[:, column(at, "A", False)], first, sems.at[0]),
        pltpu.make_async_copy(delta.at[:READ, column(at, "B", False)], second, sems.at[1]),
    ]
    for copy in copies:
        copy.start()
    out[1024 + SPLIT :, :] = jnp.full((EXTRA, 256), weight, F32)
    copies[0].wait()
    out[:1024, :] = weight * first[...].astype(F32)
    copies[1].wait()
    out[1024 : 1024 + SPLIT, :] = weight * second[...].astype(F32)[:SPLIT, :]


def pair_kernel(at, weight, delta, last, own):
    for kind, out in (("C", last), ("O", own)):
        out[:1024, :] = weight * delta[:, column(at, kind, False)].astype(F32)
        out[1024:ROWS, :] = jnp.full((EXTRA, 256), weight, F32)
    last[ROWS:, :] = weight * delta[REST:, column(at, "B", False)].astype(F32)[SPLIT - REST :, :]


def z_first_kernel(at, weight, delta, pair, first):
    first[:1024, :] = weight * delta[:, column(at, "A", True)].astype(F32) + pair[:1024, :]
    direct = weight * delta[:READ, column(at, "B", True)].astype(F32)
    first[1024 : 1024 + SPLIT, :] = direct[:SPLIT, :] + pair[1024 : 1024 + SPLIT, :]
    first[1024 + SPLIT :, :] = weight + pair[1024 + SPLIT :, :]


def z_rest_kernel(at, weight, delta, pair, rest):
    direct = weight * delta[REST:, column(at, "B", True)].astype(F32)
    rest[...] = direct[SPLIT - REST :, :] + pair[ROWS:, :]


def z_last_kernel(at, weight, delta, pair, got, last):
    total = weight * delta[:, column(at, "C", True)].astype(F32) + pair[:1024, :]
    last[:1024, :] = total + got[:1024, :]
    last[1024:, :] = weight + pair[1024:1025, :] + got[1024 + SPLIT : 1025 + SPLIT, :]


def z_own_kernel(at, weight, delta, pair, got, rest, own):
    total = weight * delta[:, column(at, "O", True)].astype(F32) + pair[:1024, :]
    own[:SPLIT, :] = total[:SPLIT, :] + got[1024 : 1024 + SPLIT, :]
    own[SPLIT:1024, :] = total[SPLIT:, :] + rest[...]
    own[1024:, :] = weight + pair[1024:, :] + got[1024 + SPLIT :, :]


def finish(parts, rows, mean, moment, outs, stores, sems):
    copies = []
    for i in range(parts):
        part = slice(i * rows, (i + 1) * rows)
        here = mean(part)
        new = 0.9 * moment[part, :] + here
        stores[0][part, :] = 0.7 * (here + 0.9 * new)
        stores[1][part, :] = new
        for k in range(2):
            copy = pltpu.make_async_copy(stores[k].at[part, :], outs[k].at[part, :], sems.at[k, i])
            copy.start()
            copies.append(copy)
    return copies


def finish_kernel(at, weight, part, last_two, moment_two, own, last, other, got, moment_one, *refs):
    outs_one, outs_two, stores_one, stores_two = refs[:2], refs[2:4], refs[4:6], refs[6:8]
    weights_two = part[1024:1025, :] + last_two[1024:1025, :]
    weights_one = jnp.concatenate([other[:, 8192:] + got[:, 8192:]] * 8, axis=1)

    def mean_two(rows):
        return (part[rows, :] + last_two[rows, :]) / weights_two

    def mean_one(rows):
        groups = [slice(128 * i, 128 * i + 1024) for i in range(rows.start, rows.stop, 8)]
        return jnp.concatenate([(own[:, g] + last[:, g] + got[:, g]) / weights_one for g in groups], axis=0)

    copies = finish(4, 256, mean_two, moment_two, outs_two, stores_two, refs[8])
    copies += finish(1, 64, mean_one, moment_one, outs_one, stores_one, refs[9])
    for copy in copies:
        copy.wait()


def product(weight, tokens, start, upstream):
    part = tokens[:, pl.ds(pl.multiple_of(start, 256), 256)]
    return weight * lax.dot_general(part, upstream[...], (((0,), (0,)), ((), ())), preferred_element_type=F32)


def y_first_kernel(kinds):
    def body(at, weight, tokens, upstream, *outs):
        for kind, out in zip(kinds, outs):
            out[:256, :] = product(weight, tokens, 1024 * (1 - at[4]) + 256 * place(at, kind, 2), upstream)
            out[256:, :] = jnp.full((1, 1024), weight, F32)

    return body


def x_first_kernel(at, weight, tokens, upstream, *refs):
    for y in range(4):
        grad = product(weight, tokens, 1024 * at[4] + 256 * y, upstream)
        for x in range(4):
            for kind, out in zip("ABCO", refs):

                @pl.when(place(at, kind, 3) == x)
                def _():
                    out[64 * y : 64 * y + 64, :] = grad[64 * x : 64 * x + 64, :]


def add_kernel(at, weight, a, b, out):
    out[...] = a[...] + b[...]


def add_two_kernel(at, weight, last, relayed, own, direct, last_out, own_out):
    last_out[...] = last[...] + relayed[...]
    own_out[...] = own[...] + direct[...]


def flat(tail):
    return (8, 8 * 1024 + 128 * tail)


def split_kernel(axis, extra):
    def body(at, weight, a, b, c, *outs):
        for kind, out in zip("ABCO", outs):
            rows = pl.ds(pl.multiple_of(64 * place(at, kind, axis), 64), 64)
            total = a[rows, :] + b[rows, :] + c[rows, :]
            for i in range(8):
                out[:, 1024 * i : 1024 * i + 1024] = total[8 * i : 8 * i + 8, :]
            shape = (8, out.shape[1] - 8192)
            if extra:
                weights = a[256:257, :128] + b[256:257, :128] + c[256:257, :128]
                out[:, 8192:] = jnp.broadcast_to(weights, shape)
            else:
                out[:, 8192:] = jnp.zeros(shape, F32)

    return body


def on_device(counts, inputs, cotangent, delta_two, moment_one, moment_two):
    delta, tokens, upstream = delta_two[0, 0], inputs[0, 0], cotangent[0, 0]
    two, y_part, x_part = (1024 + EXTRA, 256), (257, 1024), (256, 1024)
    run = lambda body, name, shapes, *arrays, **more: call(body, name, shapes, counts, *arrays, **more)

    pair_ab = run(
        first_pair_kernel,
        "pair_ab",
        [(FIRST, 256)],
        hbm=(delta,),
        scratch=[pltpu.VMEM((rows, 256), jnp.bfloat16) for rows in (1024, READ)] + [pltpu.SemaphoreType.DMA((2,))],
        limit=49,
    )
    got_ab = send(pair_ab, along("core", 1))
    ya, yb = run(y_first_kernel("AB"), "yab", [y_part] * 2, tokens, upstream, after=(pair_ab,))
    got_ya, got_yb = send(ya, forward("y")), send(yb, backward("y"))
    za = run(z_first_kernel, "zab", [(FIRST, 256)], delta, got_ab, after=(ya,))
    got_za = send(za, forward("zhi"))
    xa, xb, xc, xo = run(x_first_kernel, "x", [x_part] * 4, tokens, upstream, after=(za,))
    got_xa, got_xb = send(xa, forward("x")), send(xb, backward("x"))
    yc, yo = run(y_first_kernel("CO"), "yco", [y_part] * 2, tokens, upstream, after=(xa,))
    pair_c, pair_o = run(pair_kernel, "pair_co", [(two[0] + 1024 - SPLIT, 256), two], delta, after=(yc,))
    got_c, got_o = send(pair_c, along("core", 1)), send(pair_o, along("core", 1))
    yc = run(add_kernel, "yc", [y_part], yc, got_ya, after=(got_yb, pair_o))
    got_yc = send(yc, forward("y"))
    xc = run(add_kernel, "xc", [x_part], xc, got_xa, after=(yc, got_xb))
    got_xc = send(xc, forward("x"))
    zb = run(z_rest_kernel, "zb", [(1024 - SPLIT, 256)], delta, got_c, after=(xc,))
    got_zb = send(zb, forward("zhi"))
    zc = run(z_last_kernel, "zc", [(1025, 256)], delta, got_c, got_za, after=(zb,))
    got_zc = send(zc, lambda core: {"zhi": 1 if core == 0 else -1, "core": 1})
    zo = run(z_own_kernel, "zo", [two], delta, got_o, got_za, got_zb, after=(zc,))

    a_part, b_part = flat(2), flat(1)
    ba, bb, bc, bo = run(split_kernel(3, True), "y_sum", [b_part] * 4, yo, got_yb, got_yc, after=(zo,))
    got_ba, got_bb = send(ba, forward("x")), send(bb, backward("x"))
    aa, ab, ac, ao = run(split_kernel(2, False), "x_sum", [a_part] * 4, xo, got_xb, got_xc, after=(ba,))
    got_aa, got_ab = send(aa, forward("y")), send(ab, backward("y"))
    bc, bo = run(add_two_kernel, "bc", [b_part] * 2, bc, got_ba, bo, got_bb, after=(aa,))
    got_bc = send(bc, forward("x"))
    ac, ao = run(add_two_kernel, "ac", [a_part] * 2, ac, got_aa, ao, got_ab, after=(bc,))
    got_ac = send(ac, forward("y"))
    other = run(add_kernel, "cross", [b_part], bo, got_bc, after=(ac,))
    got = send(other, along("zlo", 1))
    step_one, moment_one_new, step_two, moment_two_new = run(
        finish_kernel,
        "finish",
        [(64, 1024)] * 2 + [(1024, 256)] * 2,
        *(zo, got_zc, moment_two[0], ao, got_ac, other, got, moment_one[0]),
        hbm_outs=4,
        scratch=[pltpu.VMEM((64, 1024), F32)] * 2
        + [pltpu.VMEM((1024, 256), F32)] * 2
        + [pltpu.SemaphoreType.DMA((2, 4)), pltpu.SemaphoreType.DMA((2, 1))],
    )
    return (step_one[None], moment_one_new[None], step_two[None], moment_two_new[None])


def solution(mesh):
    fine = Mesh(mesh.devices.reshape(SIZES), AXES)
    row, col = AXES[:3], AXES[3:]
    return jax.shard_map(
        on_device,
        mesh=fine,
        in_specs=(
            P(row, col),
            P(row, col, None, None),
            P(row, col, None, None),
            P(row, col, None, None),
            P(col, row, None),
            P(row, None, col),
        ),
        out_specs=(
            P(col, row, None),
            P(col, row, None),
            P(row, None, col),
            P(row, None, col),
        ),
        check_vma=False,
    )
```
